32 devices in a mesh: seq: 16 (over z, y, x), head: 2 (over core).
Axes of the slice: x: 2, y: 2, z: 4, core: 2. Of those that a mesh axis runs over, the one named last changes fastest.
Arguments:
- queries: bfloat16 [8192, 4096], P('seq', 'head'), may hold values from -64 to 64
- keys: bfloat16 [8192, 2048], P('seq', 'head'), may hold values from -20 to 20
- values: bfloat16 [8192, 2048], P('seq', 'head'), may hold values from -6 to 6
- start_basis: float32 [16, 128, 64], P('head'), may hold values from -6 to 6
- out_weight: bfloat16 [4096, 2688], P('head'), may hold values from -0.09375 to 0.09375
Outputs:
- lowrank_attn: bfloat16 [8192, 4096], P('seq', 'head')
- deviation: bfloat16 [8192, 2688], P(('seq', 'head'))
The draws below stay inside these ranges and needn't reach their ends.
All inputs are finite; a program needn't handle non-finite values.
Results may differ from the reference program's by a relative error of at most 0.029.
Values may be sent and summed in bfloat16 or wider, within the bound.
A program may use at most 192 MiB of HBM per device.

```python
import math
import jax
import jax.numpy as jnp
from jax import lax

HQ = 32
HK = 16
HD = 128
QSCALE = 168
W = 1024
D_WIN = 2688
RANK = 64
SWEEPS = 8
TOK_DEV = 512
TOKENS = 8192
QH_DEV = 16
N_SEQ = 16
N_HEAD = 2


def key_field(key):
    base_key = jax.random.fold_in(key, 7301)
    key_raw, key_order, key_top, key_bottom, key_mix, key_rough = jax.random.split(base_key, 6)
    raw = jnp.clip(jax.random.normal(key_raw, (TOKENS, HK, HD), jnp.float32), -5.0, 5.0)
    order = jax.vmap(lambda single: jax.random.permutation(single, HD))(jax.random.split(key_order, HK))
    top_spread = jax.random.uniform(key_top, (HK, HD), jnp.float32, 1.0, 1.6)
    bottom_spread = jax.random.uniform(key_bottom, (HK, HD), jnp.float32, 0.55, 0.95)
    spread = jnp.where(order < RANK, top_spread, bottom_spread)
    mixing = jnp.eye(HD, dtype=jnp.float32)[None] + 0.5 / math.sqrt(HD) * jax.random.normal(key_mix, (HK, HD, HD), jnp.float32)
    ramp = 0.6 + 1.2 * jnp.arange(TOKENS, dtype=jnp.float32) / TOKENS
    rough = jnp.exp(jax.random.uniform(key_rough, (TOKENS,), jnp.float32, -0.4, 0.4))
    scaled = raw * spread[None] * (ramp * rough)[:, None, None]
    field = jnp.einsum('thc,hcd->thd', scaled, mixing, precision=lax.Precision.HIGHEST)
    return jnp.clip(field, -20.0, 20.0)


def draw_keys(key, part):
    return key_field(key).reshape(TOKENS, HK * HD).astype(jnp.bfloat16)


def draw_queries(key, part):
    query_key = jax.random.fold_in(key, 9113)
    group_q = HQ // HK
    result = jax.random.normal(query_key, (TOKENS, HK, group_q, HD), jnp.float32)
    return jnp.clip(result, -64.0, 64.0).reshape(TOKENS, HQ * HD).astype(jnp.bfloat16)


def shard_levels(own_key, extent, cuts, low, largest):
    loudness = 1.0
    for axis_at, blocks in cuts:
        heights = jax.random.uniform(jax.random.fold_in(jax.random.fold_in(own_key, 6), axis_at), (blocks,), jnp.float32, low / len(cuts), largest / len(cuts))
        loudness = loudness * jnp.repeat(jnp.exp(heights), extent[axis_at] // blocks).reshape((-1,) + (1,) * (len(extent) - 1 - axis_at))
    return loudness


def noise(own_key, extent, deviation, reach, cuts=(), kind=jnp.bfloat16):
    drawn = jax.random.normal(own_key, extent, jnp.float32) * deviation
    if len(cuts) > 0:
        drawn = shard_levels(own_key, extent, cuts, -0.22, 0.18) * drawn
    return jnp.clip(drawn, min=-reach, max=reach).astype(kind)


def setup_inputs(seed: int = 0) -> dict:
    key_list = jax.random.split(jax.random.key(seed), 6)
    return {
        "queries": draw_queries(jax.random.fold_in(key_list[5], 71), 0),
        "keys": draw_keys(jax.random.fold_in(key_list[5], 71), 0),
        "values": noise(key_list[2], (TOKENS, HK * HD), 1.0, 6.0, ((0, 16), (1, 2))),
        "start_basis": noise(key_list[3], (HK, HD, RANK), 1.0, 6.0, ((0, 2),), jnp.float32),
        "out_weight": noise(key_list[4], (HQ * HD, D_WIN), (HQ * HD) ** -0.5, 0.09375, ((0, 2),)),
    }


HIGHEST = lax.Precision.HIGHEST
NEGLIGIBLE = -1e+30

def orthonormal(columns):
    inner_prod = jnp.einsum('hcr,hcq->hrq', columns, columns, precision=HIGHEST)
    factor_low = jnp.linalg.cholesky(inner_prod)

    def solve_one(factor, column):
        return jax.scipy.linalg.solve_triangular(factor, column.T, lower=True).T
    return jax.vmap(solve_one)(factor_low, columns)

def attend(query_rows, key_rows, value_rows, first_pos, score_scale):
    row_count = query_rows.shape[0]
    key_span = key_rows.shape[0]
    query_pos = first_pos + jnp.arange(row_count, dtype=jnp.int32)
    key_pos = first_pos + row_count - key_span + jnp.arange(key_span, dtype=jnp.int32)
    allowed = (key_pos[None, :] >= 0) & (key_pos[None, :] <= query_pos[:, None]) & (query_pos[:, None] - key_pos[None, :] < W)
    scores = jnp.einsum('thgd,shd->hgts', query_rows.astype(jnp.float32), key_rows.astype(jnp.float32), precision=HIGHEST) * score_scale
    scores = jnp.where(allowed, scores, NEGLIGIBLE)
    row_peak = jnp.max(scores, axis=-1, keepdims=True)
    raised = jnp.exp(scores - row_peak)
    weights = (raised / jnp.sum(raised, axis=-1, keepdims=True)).astype(jnp.bfloat16)
    return jnp.einsum('hgts,shd->thgd', weights.astype(jnp.float32), value_rows.astype(jnp.float32), precision=HIGHEST)

def reference(queries, keys, values, start_basis, out_weight):
    group_q = HQ // HK
    score_scale = QSCALE ** (-0.5)
    key_heads = keys.reshape(TOKENS, HK, HD)
    value_heads = values.reshape(TOKENS, HK, HD)
    query_heads = queries.reshape(TOKENS, HK, group_q, HD)
    key_float = key_heads.astype(jnp.float32)
    key_gram = jnp.einsum('thc,thd->hcd', key_float, key_float, precision=HIGHEST)
    basis = start_basis
    for sweep in range(SWEEPS):
        basis = orthonormal(jnp.einsum('hcd,hdr->hcr', key_gram, basis, precision=HIGHEST))
    basis_half = basis.astype(jnp.bfloat16)
    query_low = jnp.einsum('thgc,hcr->thgr', query_heads.astype(jnp.float32), basis_half.astype(jnp.float32), precision=HIGHEST).astype(jnp.bfloat16)
    key_low = jnp.einsum('thc,hcr->thr', key_float, basis_half.astype(jnp.float32), precision=HIGHEST).astype(jnp.bfloat16)
    key_pad = jnp.concatenate([jnp.zeros((W, HK, HD), jnp.bfloat16), key_heads], axis=0)
    low_pad = jnp.concatenate([jnp.zeros((W, HK, RANK), jnp.bfloat16), key_low], axis=0)
    value_pad = jnp.concatenate([jnp.zeros((W, HK, HD), jnp.bfloat16), value_heads], axis=0)

    def one_block(index):
        first_pos = (index * TOK_DEV).astype(jnp.int32)
        query_rows = lax.dynamic_slice_in_dim(query_heads, first_pos, TOK_DEV, 0)
        query_lrows = lax.dynamic_slice_in_dim(query_low, first_pos, TOK_DEV, 0)
        key_rows = lax.dynamic_slice_in_dim(key_pad, first_pos, W + TOK_DEV, 0)
        key_lrows = lax.dynamic_slice_in_dim(low_pad, first_pos, W + TOK_DEV, 0)
        value_rows = lax.dynamic_slice_in_dim(value_pad, first_pos, W + TOK_DEV, 0)
        exact = attend(query_rows, key_rows, value_rows, first_pos, score_scale)
        approx = attend(query_lrows, key_lrows, value_rows, first_pos, score_scale)
        return (approx.astype(jnp.bfloat16), (exact - approx).astype(jnp.bfloat16))
    approx_all, gap_all = lax.map(one_block, jnp.arange(N_SEQ, dtype=jnp.int32))
    lowrank_attn = approx_all.reshape(TOKENS, HQ * HD)
    gap = gap_all.reshape(TOKENS, HQ * HD)
    group_width = QH_DEV * HD
    total = jnp.zeros((TOKENS, D_WIN), jnp.float32)
    for group in range(N_HEAD):
        partial_value = jnp.dot(gap[:, group * group_width:(group + 1) * group_width].astype(jnp.float32), out_weight[group * group_width:(group + 1) * group_width].astype(jnp.float32), preferred_element_type=jnp.float32).astype(jnp.bfloat16)
        partial_value = lax.optimization_barrier(partial_value)
        total = total + partial_value.astype(jnp.float32)
    return (lowrank_attn, total.astype(jnp.bfloat16))
```

```python
import functools
import math

import jax
import jax.numpy as jnp
from jax import lax
from jax.experimental import pallas as pl
from jax.experimental.pallas import tpu as pltpu
from jax.sharding import PartitionSpec as P

HQ = 32
HK = 16
HD = 128
QSCALE = 168
W = 1024
SWEEPS = 8
GROUP = HQ // HK
TILE = 128
PAIR = 2

HIGHEST = lax.Precision.HIGHEST
NEGLIGIBLE = -1e30
F32 = jnp.float32
BF16 = jnp.bfloat16


def from_behind(array, axis, by):
    peers = lax.axis_size(axis)
    pairs = [(i, i + by) for i in range(peers) if 0 <= i + by < peers]
    return lax.ppermute(array, axis, pairs)


def dot(a, b, dims, precision=None):
    return lax.dot_general(
        a, b, (dims, ((), ())), precision=precision, preferred_element_type=F32
    )


def gram_kernel(keys_ref, gram_ref):
    for head in range(gram_ref.shape[0]):
        block = keys_ref[:, head * HD:(head + 1) * HD]
        gram_ref[head] = dot(block, block, ((0,), (0,)))


def eliminate(work, heads, rank):
    for k in range(0, rank, PAIR):
        rows = [work[k + j] for j in range(PAIR)]
        corner = [[rows[j][:, k + m:k + m + 1] for m in range(PAIR)] for j in range(PAIR)]
        ratio = [[None] * PAIR for _ in range(PAIR)]
        scaled = []
        for j in range(PAIR):
            inverse = 1.0 / corner[j][j]
            scaled.append(rows[j] * inverse)
            for m in range(j + 1, PAIR):
                ratio[j][m] = corner[j][m] * inverse
            for l in range(j + 1, PAIR):
                rows[l] = rows[l] - corner[l][j] * scaled[j]
                for m in range(j + 1, PAIR):
                    corner[l][m] = corner[l][m] - corner[l][j] * ratio[j][m]
        for j in range(PAIR):
            work[k + j] = rows[j] * lax.rsqrt(corner[j][j])
        if k + PAIR < rank:
            rest = work[k + PAIR:]
            factors = [rest[:, :, k + m:k + m + 1] for m in range(PAIR)]
            for j in range(PAIR):
                for m in range(j + 1, PAIR):
                    factors[m] = factors[m] - factors[j] * ratio[j][m][None]
                rest = rest - factors[j] * scaled[j][None]
            work[k + PAIR:] = rest


def basis_kernel(gram_ref, start_ref, half_ref, basis, product, work):
    heads, _, rank = start_ref.shape
    basis[...] = start_ref[...]
    lane = lax.broadcasted_iota(jnp.int32, (rank, rank), 1)
    unit = jnp.where(lax.broadcasted_iota(jnp.int32, (rank, rank), 0) == lane, 1.0, 0.0)

    def sweep(_, carry):
        for head in range(heads):
            z = dot(gram_ref[head], basis[head], ((1,), (0,)), HIGHEST)
            product[head] = z
            inner = dot(z, z, ((0,), (0,)), HIGHEST)
            work[:, head, :] = jnp.concatenate([inner, unit], axis=1)
        eliminate(work, heads, rank)
        for head in range(heads):
            inverse = work[:, head, :][:, rank:]
            basis[head] = dot(product[head], inverse, ((1,), (1,)), HIGHEST)
        return carry

    lax.fori_loop(0, SWEEPS, sweep, 0)
    half_ref[...] = basis[...].astype(BF16)


def soft(queries, keys, values, low_mask, high_mask):
    scores = dot(queries, keys, ((1,), (1,)))
    scores = jnp.concatenate(
        [
            jnp.where(low_mask, scores[:, :TILE], NEGLIGIBLE),
            scores[:, TILE:-TILE],
            jnp.where(high_mask, scores[:, -TILE:], NEGLIGIBLE),
        ],
        axis=1,
    )
    peak = jnp.max(scores, axis=-1, keepdims=True)
    raised = jnp.exp2((scores - peak) * (QSCALE ** (-0.5) * math.log2(math.e)))
    both = dot(raised.astype(BF16), values, ((1,), (0,)))
    return both[:, :HD] / both[:, HD:]


def attend_kernel(prior, *refs):
    query_ref = refs[0]
    key_refs = refs[1:prior + 2]
    value_refs = refs[prior + 2:2 * prior + 3]
    half_ref, low_ref, gap_ref, window_k, window_v, window_low = refs[2 * prior + 3:]
    rows = query_ref.shape[0]
    where_at = lax.axis_index("seq")
    first = key_refs[prior][0:1, :]
    for distance in range(1, prior + 1):
        first = jnp.where(where_at >= distance, key_refs[prior - distance][0:1, :], first)
    for block in range(prior + 1):
        real = where_at >= prior - block
        part = pl.ds(block * rows, rows)
        window_k[part, :] = jnp.where(real, key_refs[block][...], first)
        window_v[part, :HD] = value_refs[block][...]
        window_v[part, HD:] = jnp.where(
            real, jnp.ones((rows, HD), BF16), jnp.zeros((rows, HD), BF16)
        )
    half = half_ref[0]
    window_low[...] = dot(window_k[...], half, ((1,), (0,))).astype(BF16)
    row = lax.broadcasted_iota(jnp.int32, (TILE, TILE), 0)
    column = lax.broadcasted_iota(jnp.int32, (TILE, TILE), 1)
    low_mask = jnp.concatenate([column > row] * GROUP, axis=0)
    high_mask = jnp.concatenate([column <= row] * GROUP, axis=0)
    for start in range(0, rows, TILE):
        queries = jnp.concatenate(
            [query_ref[start:start + TILE, g * HD:(g + 1) * HD] for g in range(GROUP)], axis=0
        )
        low_queries = dot(queries, half, ((1,), (0,))).astype(BF16)
        part = pl.ds(start, W + TILE)
        values = window_v[part, :]
        exact = soft(queries, window_k[part, :], values, low_mask, high_mask)
        approx = soft(low_queries, window_low[part, :], values, low_mask, high_mask)
        gap = (exact - approx).astype(BF16)
        approx = approx.astype(BF16)
        for g in range(GROUP):
            low_ref[start:start + TILE, g * HD:(g + 1) * HD] = approx[g * TILE:(g + 1) * TILE]
            gap_ref[start:start + TILE, g * HD:(g + 1) * HD] = gap[g * TILE:(g + 1) * TILE]


def shards(queries, keys, values, start_basis, out_weight):
    tok_rows = keys.shape[0]
    heads, _, rank = start_basis.shape
    prior = W // tok_rows
    local_gram = pl.pallas_call(
        gram_kernel,
        out_shape=jax.ShapeDtypeStruct((heads, HD, HD), F32),
        compiler_params=pltpu.CompilerParams(vmem_limit_bytes=24 << 20),
        cost_estimate=pl.CostEstimate(
            flops=2 * tok_rows * HD * HD * heads, bytes_accessed=2 << 20, transcendentals=0
        ),
        name="gram",
    )(keys)
    key_gram = lax.psum(local_gram, "seq")
    key_blocks = [from_behind(keys, "seq", d) for d in range(prior, 0, -1)] + [keys]
    value_blocks = [from_behind(values, "seq", d) for d in range(prior, 0, -1)] + [values]
    basis_half = pl.pallas_call(
        basis_kernel,
        out_shape=jax.ShapeDtypeStruct((heads, HD, rank), BF16),
        scratch_shapes=[
            pltpu.VMEM((heads, HD, rank), F32),
            pltpu.VMEM((heads, HD, rank), F32),
            pltpu.VMEM((rank, heads, 2 * rank), F32),
        ],
        compiler_params=pltpu.CompilerParams(vmem_limit_bytes=24 << 20),
        cost_estimate=pl.CostEstimate(
            flops=40_000_000_000, bytes_accessed=2 << 20, transcendentals=0
        ),
        name="basis",
    )(key_gram, start_basis)

    wide = pl.BlockSpec((tok_rows, GROUP * HD), lambda h: (0, h))
    narrow = pl.BlockSpec((tok_rows, HD), lambda h: (0, h))
    span = (prior + 1) * tok_rows
    lowrank_attn, gap = pl.pallas_call(
        functools.partial(attend_kernel, prior),
        grid=(heads,),
        in_specs=[wide]
        + [narrow] * (2 * prior + 2)
        + [pl.BlockSpec((1, HD, rank), lambda h: (h, 0, 0))],
        out_specs=[wide, wide],
        out_shape=[jax.ShapeDtypeStruct(queries.shape, BF16)] * 2,
        scratch_shapes=[
            pltpu.VMEM((span, HD), BF16),
            pltpu.VMEM((span, 2 * HD), BF16),
            pltpu.VMEM((span, rank), BF16),
        ],
        compiler_params=pltpu.CompilerParams(vmem_limit_bytes=48 << 20),
        cost_estimate=pl.CostEstimate(
            flops=30_000_000_000, bytes_accessed=16 << 20, transcendentals=40_000_000
        ),
        name="attend",
    )(queries, *key_blocks, *value_blocks, basis_half)

    peers = lax.axis_size("head")
    if peers == 2:
        mine = lax.axis_index("head")
        half_rows = tok_rows // 2

        def project(which):
            rows = lax.dynamic_slice_in_dim(gap, which * half_rows, half_rows, 0)
            return jnp.dot(rows, out_weight, preferred_element_type=F32).astype(BF16)

        arrived = lax.ppermute(project(1 - mine), "head", [(0, 1), (1, 0)])
        deviation = (project(mine).astype(F32) + arrived.astype(F32)).astype(BF16)
    else:
        deviation = lax.psum_scatter(
            jnp.dot(gap, out_weight, preferred_element_type=F32).astype(BF16),
            "head",
            scatter_dimension=0,
            tiled=True,
        )
    return (lowrank_attn, deviation)


def solution(mesh):
    placed = (
        P("seq", "head"),
        P("seq", "head"),
        P("seq", "head"),
        P("head", None, None),
        P("head", None),
    )
    return jax.shard_map(
        shards,
        mesh=mesh,
        in_specs=placed,
        out_specs=(P("seq", "head"), P(("seq", "head"), None)),
        check_vma=False,
    )
```

```python
import functools
import math

import jax
import jax.numpy as jnp
from jax import lax
from jax.experimental import pallas as pl
from jax.experimental.pallas import tpu as pltpu
from jax.sharding import PartitionSpec as P

HQ = 32
HK = 16
HD = 128
QSCALE = 168
W = 1024
SWEEPS = 8
GROUP = HQ // HK
TILE = 128
STEP = 4
SUB = 8

HIGHEST = lax.Precision.HIGHEST
NEGLIGIBLE = -1e30
F32 = jnp.float32
BF16 = jnp.bfloat16


def from_behind(array, axis, by):
    peers = lax.axis_size(axis)
    pairs = [(i, i + by) for i in range(peers) if 0 <= i + by < peers]
    return lax.ppermute(array, axis, pairs)


def dot(a, b, dims, precision=None):
    return lax.dot_general(
        a, b, (dims, ((), ())), precision=precision, preferred_element_type=F32
    )


def gram_kernel(keys_ref, gram_ref):
    for head in range(gram_ref.shape[0]):
        block = keys_ref[:, head * HD:(head + 1) * HD]
        gram_ref[head] = dot(block, block, ((0,), (0,)))


def inverse_factor(inner, unit):
    rank = inner.shape[0]
    whole = jnp.concatenate([inner, unit], axis=1)
    width = whole.shape[1]
    blocks = [whole[at:at + SUB] for at in range(0, rank, SUB)]
    level = lax.broadcasted_iota(jnp.int32, (SUB, width), 0)
    for k in range(0, rank, STEP):
        own, inside = k // SUB, k % SUB
        rows = [
            jnp.broadcast_to(blocks[own][inside + j:inside + j + 1], (SUB, width))
            for j in range(STEP)
        ]
        corner = [
            [
                jnp.broadcast_to(rows[j][:, k + m:k + m + 1], (SUB, width))
                for m in range(STEP)
            ]
            for j in range(STEP)
        ]
        ratio = [[None] * STEP for _ in range(STEP)]
        scaled = []
        for j in range(STEP):
            inverse = 1.0 / corner[j][j]
            scaled.append(rows[j] * inverse)
            for m in range(j + 1, STEP):
                ratio[j][m] = corner[j][m] * inverse
            for l in range(j + 1, STEP):
                rows[l] = rows[l] - corner[l][j] * scaled[j]
                for m in range(j + 1, STEP):
                    corner[l][m] = corner[l][m] - corner[l][j] * ratio[j][m]
        for at in range(own, len(blocks)):
            block = blocks[at]
            if at > own or inside + STEP < SUB:
                factors = [
                    jnp.broadcast_to(block[:, k + m:k + m + 1], (SUB, width))
                    for m in range(STEP)
                ]
                for j in range(STEP):
                    for m in range(j + 1, STEP):
                        factors[m] = factors[m] - factors[j] * ratio[j][m]
                    block = block - factors[j] * scaled[j]
            if at == own:
                block = jnp.where(level < inside, blocks[own], block)
                for j in range(STEP):
                    done = rows[j] * lax.rsqrt(corner[j][j])
                    block = jnp.where(level == inside + j, done, block)
            blocks[at] = block
    return jnp.concatenate(blocks, axis=0)[:, rank:]


def basis_kernel(gram_ref, start_ref, half_ref, basis):
    rank = start_ref.shape[2]
    basis[...] = start_ref[0]
    lane = lax.broadcasted_iota(jnp.int32, (rank, rank), 1)
    unit = jnp.where(lax.broadcasted_iota(jnp.int32, (rank, rank), 0) == lane, 1.0, 0.0)

    def sweep(_, carry):
        z = dot(gram_ref[0], basis[...], ((1,), (0,)), HIGHEST)
        inner = dot(z, z, ((0,), (0,)), HIGHEST)
        basis[...] = dot(z, inverse_factor(inner, unit), ((1,), (1,)), HIGHEST)
        return carry

    lax.fori_loop(0, SWEEPS, sweep, 0)
    half_ref[0] = basis[...].astype(BF16)


def subspace(gram, start):
    heads, _, rank = start.shape
    return pl.pallas_call(
        basis_kernel,
        grid=(heads,),
        in_specs=[
            pl.BlockSpec((1, HD, HD), lambda h: (h, 0, 0)),
            pl.BlockSpec((1, HD, rank), lambda h: (h, 0, 0)),
        ],
        out_specs=pl.BlockSpec((1, HD, rank), lambda h: (h, 0, 0)),
        out_shape=jax.ShapeDtypeStruct((heads, HD, rank), BF16),
        scratch_shapes=[pltpu.VMEM((HD, rank), F32)],
        compiler_params=pltpu.CompilerParams(vmem_limit_bytes=24 << 20),
        cost_estimate=pl.CostEstimate(
            flops=40_000_000_000, bytes_accessed=2 << 20, transcendentals=0
        ),
        name="basis",
    )(gram, start)


def partner(array, axis, mask):
    return lax.ppermute(array, axis, [(i, i ^ mask) for i in range(lax.axis_size(axis))])


def soft(queries, keys, values, low_mask, high_mask):
    scores = dot(queries, keys, ((1,), (1,)))
    scores = jnp.concatenate(
        [
            jnp.where(low_mask, scores[:, :TILE], NEGLIGIBLE),
            scores[:, TILE:-TILE],
            jnp.where(high_mask, scores[:, -TILE:], NEGLIGIBLE),
        ],
        axis=1,
    )
    peak = jnp.max(scores, axis=-1, keepdims=True)
    raised = jnp.exp2((scores - peak) * (QSCALE ** (-0.5) * math.log2(math.e)))
    both = dot(raised.astype(BF16), values, ((1,), (0,)))
    return both[:, :HD] / both[:, HD:]


def attend_kernel(prior, *refs):
    query_ref = refs[0]
    key_refs = refs[1:prior + 2]
    value_refs = refs[prior + 2:2 * prior + 3]
    half_ref, low_ref, gap_ref, window_k, window_v, window_low = refs[2 * prior + 3:]
    rows = query_ref.shape[0]
    where_at = lax.axis_index("seq")
    first = key_refs[prior][0:1, :]
    for distance in range(1, prior + 1):
        first = jnp.where(where_at >= distance, key_refs[prior - distance][0:1, :], first)
    for block in range(prior + 1):
        real = where_at >= prior - block
        part = pl.ds(block * rows, rows)
        window_k[part, :] = jnp.where(real, key_refs[block][...], first)
        window_v[part, :HD] = value_refs[block][...]
        window_v[part, HD:] = jnp.where(
            real, jnp.ones((rows, HD), BF16), jnp.zeros((rows, HD), BF16)
        )
    half = half_ref[0]
    window_low[...] = dot(window_k[...], half, ((1,), (0,))).astype(BF16)
    row = lax.broadcasted_iota(jnp.int32, (TILE, TILE), 0)
    column = lax.broadcasted_iota(jnp.int32, (TILE, TILE), 1)
    low_mask = jnp.concatenate([column > row] * GROUP, axis=0)
    high_mask = jnp.concatenate([column <= row] * GROUP, axis=0)
    for start in range(0, rows, TILE):
        queries = jnp.concatenate(
            [query_ref[start:start + TILE, g * HD:(g + 1) * HD] for g in range(GROUP)], axis=0
        )
        low_queries = dot(queries, half, ((1,), (0,))).astype(BF16)
        part = pl.ds(start, W + TILE)
        values = window_v[part, :]
        exact = soft(queries, window_k[part, :], values, low_mask, high_mask)
        approx = soft(low_queries, window_low[part, :], values, low_mask, high_mask)
        gap = (exact - approx).astype(BF16)
        approx = approx.astype(BF16)
        for g in range(GROUP):
            low_ref[start:start + TILE, g * HD:(g + 1) * HD] = approx[g * TILE:(g + 1) * TILE]
            gap_ref[start:start + TILE, g * HD:(g + 1) * HD] = gap[g * TILE:(g + 1) * TILE]


def shards(queries, keys, values, start_basis, out_weight):
    tok_rows = keys.shape[0]
    heads, _, rank = start_basis.shape
    prior = W // tok_rows
    local_gram = pl.pallas_call(
        gram_kernel,
        out_shape=jax.ShapeDtypeStruct((heads, HD, HD), F32),
        compiler_params=pltpu.CompilerParams(vmem_limit_bytes=24 << 20),
        cost_estimate=pl.CostEstimate(
            flops=2 * tok_rows * HD * HD * heads, bytes_accessed=2 << 20, transcendentals=0
        ),
        name="gram",
    )(keys)
    peers = lax.axis_size("seq")
    where_at = lax.axis_index("seq")
    spread = peers >= heads and peers & (peers - 1) == 0 and heads & (heads - 1) == 0
    if spread:
        total, left, bit = local_gram, heads, 1
        while bit < peers:
            if left > 1:
                left //= 2
                upper = (where_at & bit) != 0
                sent = jnp.where(upper, total[:left], total[left:])
                total = jnp.where(upper, total[left:], total[:left]) + partner(sent, "seq", bit)
            else:
                total = total + partner(total, "seq", bit)
            bit *= 2
        total, keys, values = lax.optimization_barrier((total, keys, values))
    else:
        total = lax.psum(local_gram, "seq")
    key_blocks = [from_behind(keys, "seq", d) for d in range(prior, 0, -1)] + [keys]
    value_blocks = [from_behind(values, "seq", d) for d in range(prior, 0, -1)] + [values]
    if spread:
        owner, left, bit = 0, heads, 1
        while left > 1:
            left //= 2
            owner = owner + jnp.where((where_at & bit) != 0, left, 0)
            bit *= 2
        start = lax.dynamic_slice_in_dim(start_basis, owner, 1, 0)
        basis_half = subspace(total, start)
        while bit > 1:
            bit //= 2
            upper = (where_at & bit) != 0
            other = partner(basis_half, "seq", bit)
            basis_half = jnp.concatenate(
                [jnp.where(upper, other, basis_half), jnp.where(upper, basis_half, other)], axis=0
            )
    else:
        basis_half = subspace(total, start_basis)

    wide = pl.BlockSpec((tok_rows, GROUP * HD), lambda h: (0, h))
    narrow = pl.BlockSpec((tok_rows, HD), lambda h: (0, h))
    span = (prior + 1) * tok_rows
    lowrank_attn, gap = pl.pallas_call(
        functools.partial(attend_kernel, prior),
        grid=(heads,),
        in_specs=[wide]
        + [narrow] * (2 * prior + 2)
        + [pl.BlockSpec((1, HD, rank), lambda h: (h, 0, 0))],
        out_specs=[wide, wide],
        out_shape=[jax.ShapeDtypeStruct(queries.shape, BF16)] * 2,
        scratch_shapes=[
            pltpu.VMEM((span, HD), BF16),
            pltpu.VMEM((span, 2 * HD), BF16),
            pltpu.VMEM((span, rank), BF16),
        ],
        compiler_params=pltpu.CompilerParams(vmem_limit_bytes=48 << 20),
        cost_estimate=pl.CostEstimate(
            flops=30_000_000_000, bytes_accessed=16 << 20, transcendentals=40_000_000
        ),
        name="attend",
    )(queries, *key_blocks, *value_blocks, basis_half)

    peers = lax.axis_size("head")
    if peers == 2:
        mine = lax.axis_index("head")
        half_rows = tok_rows // 2

        def project(which):
            rows = lax.dynamic_slice_in_dim(gap, which * half_rows, half_rows, 0)
            return jnp.dot(rows, out_weight, preferred_element_type=F32).astype(BF16)

        arrived = lax.ppermute(project(1 - mine), "head", [(0, 1), (1, 0)])
        deviation = (project(mine).astype(F32) + arrived.astype(F32)).astype(BF16)
    else:
        deviation = lax.psum_scatter(
            jnp.dot(gap, out_weight, preferred_element_type=F32).astype(BF16),
            "head",
            scatter_dimension=0,
            tiled=True,
        )
    return (lowrank_attn, deviation)


def solution(mesh):
    placed = (
        P("seq", "head"),
        P("seq", "head"),
        P("seq", "head"),
        P("head", None, None),
        P("head", None),
    )
    return jax.shard_map(
        shards,
        mesh=mesh,
        in_specs=placed,
        out_specs=(P("seq", "head"), P(("seq", "head"), None)),
        check_vma=False,
    )
```

```python
import functools
import math

import jax
import jax.numpy as jnp
from jax import lax
from jax.experimental import pallas as pl
from jax.experimental.pallas import tpu as pltpu
from jax.sharding import PartitionSpec as P

HQ = 32
HK = 16
HD = 128
QSCALE = 168
W = 1024
SWEEPS = 8
GROUP = HQ // HK
TILE = 128
STEP = 4
SUB = 8

HIGHEST = lax.Precision.HIGHEST
NEGLIGIBLE = -1e30
F32 = jnp.float32
BF16 = jnp.bfloat16


def from_behind(array, axis, by):
    peers = lax.axis_size(axis)
    pairs = [(i, i + by) for i in range(peers) if 0 <= i + by < peers]
    return lax.ppermute(array, axis, pairs)


def dot(a, b, dims, precision=None):
    return lax.dot_general(
        a, b, (dims, ((), ())), precision=precision, preferred_element_type=F32
    )


def gram_kernel(keys_ref, gram_ref):
    for head in range(gram_ref.shape[0]):
        block = keys_ref[:, head * HD:(head + 1) * HD]
        gram_ref[head] = dot(block, block, ((0,), (0,)))


def inverse_factor(inner, unit):
    rank = inner.shape[0]
    whole = jnp.concatenate([inner, unit], axis=1)
    width = whole.shape[1]
    blocks = [whole[at:at + SUB] for at in range(0, rank, SUB)]
    level = lax.broadcasted_iota(jnp.int32, (SUB, width), 0)
    for k in range(0, rank, STEP):
        own, inside = k // SUB, k % SUB
        rows = [
            jnp.broadcast_to(blocks[own][inside + j:inside + j + 1], (SUB, width))
            for j in range(STEP)
        ]
        corner = [
            [
                jnp.broadcast_to(rows[j][:, k + m:k + m + 1], (SUB, width))
                for m in range(STEP)
            ]
            for j in range(STEP)
        ]
        ratio = [[None] * STEP for _ in range(STEP)]
        scaled = []
        for j in range(STEP):
            inverse = 1.0 / corner[j][j]
            scaled.append(rows[j] * inverse)
            for m in range(j + 1, STEP):
                ratio[j][m] = corner[j][m] * inverse
            for l in range(j + 1, STEP):
                rows[l] = rows[l] - corner[l][j] * scaled[j]
                for m in range(j + 1, STEP):
                    corner[l][m] = corner[l][m] - corner[l][j] * ratio[j][m]
        for at in range(own, len(blocks)):
            block = blocks[at]
            if at > own or inside + STEP < SUB:
                factors = [
                    jnp.broadcast_to(block[:, k + m:k + m + 1], (SUB, width))
                    for m in range(STEP)
                ]
                for j in range(STEP):
                    for m in range(j + 1, STEP):
                        factors[m] = factors[m] - factors[j] * ratio[j][m]
                    block = block - factors[j] * scaled[j]
            if at == own:
                block = jnp.where(level < inside, blocks[own], block)
                for j in range(STEP):
                    done = rows[j] * lax.rsqrt(corner[j][j])
                    block = jnp.where(level == inside + j, done, block)
            blocks[at] = block
    return jnp.concatenate(blocks, axis=0)[:, rank:]


def basis_kernel(gram_ref, start_ref, half_ref, basis):
    rank = start_ref.shape[2]
    basis[...] = start_ref[0]
    lane = lax.broadcasted_iota(jnp.int32, (rank, rank), 1)
    unit = jnp.where(lax.broadcasted_iota(jnp.int32, (rank, rank), 0) == lane, 1.0, 0.0)

    def sweep(_, carry):
        z = dot(gram_ref[0], basis[...], ((1,), (0,)), HIGHEST)
        inner = dot(z, z, ((0,), (0,)), HIGHEST)
        basis[...] = dot(z, inverse_factor(inner, unit), ((1,), (1,)), HIGHEST)
        return carry

    lax.fori_loop(0, SWEEPS, sweep, 0)
    half_ref[0] = basis[...].astype(BF16)


def subspace(gram, start):
    heads, _, rank = start.shape
    return pl.pallas_call(
        basis_kernel,
        grid=(heads,),
        in_specs=[
            pl.BlockSpec((1, HD, HD), lambda h: (h, 0, 0)),
            pl.BlockSpec((1, HD, rank), lambda h: (h, 0, 0)),
        ],
        out_specs=pl.BlockSpec((1, HD, rank), lambda h: (h, 0, 0)),
        out_shape=jax.ShapeDtypeStruct((heads, HD, rank), BF16),
        scratch_shapes=[pltpu.VMEM((HD, rank), F32)],
        compiler_params=pltpu.CompilerParams(vmem_limit_bytes=24 << 20),
        cost_estimate=pl.CostEstimate(
            flops=40_000_000_000, bytes_accessed=2 << 20, transcendentals=0
        ),
        name="basis",
    )(gram, start)


def partner(array, axis, mask):
    return lax.ppermute(array, axis, [(i, i ^ mask) for i in range(lax.axis_size(axis))])


def soft(queries, keys, values, low_mask, high_mask):
    scores = dot(queries, keys, ((1,), (1,)))
    scores = jnp.concatenate(
        [
            jnp.where(low_mask, scores[:, :TILE], NEGLIGIBLE),
            scores[:, TILE:-TILE],
            jnp.where(high_mask, scores[:, -TILE:], NEGLIGIBLE),
        ],
        axis=1,
    )
    peak = jnp.max(scores, axis=-1, keepdims=True)
    raised = jnp.exp2((scores - peak) * (QSCALE ** (-0.5) * math.log2(math.e)))
    both = dot(raised.astype(BF16), values, ((1,), (0,)))
    return both[:, :HD] / both[:, HD:]


def attend_kernel(prior, *refs):
    query_ref = refs[0]
    key_refs = refs[1:prior + 2]
    value_refs = refs[prior + 2:2 * prior + 3]
    half_ref, low_ref, gap_ref, window_k, window_v, window_low = refs[2 * prior + 3:]
    rows = query_ref.shape[0]
    where_at = lax.axis_index("seq")
    first = key_refs[prior][0:1, :]
    for distance in range(1, prior + 1):
        first = jnp.where(where_at >= distance, key_refs[prior - distance][0:1, :], first)
    for block in range(prior + 1):
        real = where_at >= prior - block
        part = pl.ds(block * rows, rows)
        window_k[part, :] = jnp.where(real, key_refs[block][...], first)
        window_v[part, :HD] = value_refs[block][...]
        window_v[part, HD:] = jnp.where(
            real, jnp.ones((rows, HD), BF16), jnp.zeros((rows, HD), BF16)
        )
    half = half_ref[0]
    window_low[...] = dot(window_k[...], half, ((1,), (0,))).astype(BF16)
    row = lax.broadcasted_iota(jnp.int32, (TILE, TILE), 0)
    column = lax.broadcasted_iota(jnp.int32, (TILE, TILE), 1)
    low_mask = jnp.concatenate([column > row] * GROUP, axis=0)
    high_mask = jnp.concatenate([column <= row] * GROUP, axis=0)
    for start in range(0, rows, TILE):
        queries = jnp.concatenate(
            [query_ref[start:start + TILE, g * HD:(g + 1) * HD] for g in range(GROUP)], axis=0
        )
        low_queries = dot(queries, half, ((1,), (0,))).astype(BF16)
        part = pl.ds(start, W + TILE)
        values = window_v[part, :]
        exact = soft(queries, window_k[part, :], values, low_mask, high_mask)
        approx = soft(low_queries, window_low[part, :], values, low_mask, high_mask)
        gap = (exact - approx).astype(BF16)
        approx = approx.astype(BF16)
        for g in range(GROUP):
            low_ref[start:start + TILE, g * HD:(g + 1) * HD] = approx[g * TILE:(g + 1) * TILE]
            gap_ref[start:start + TILE, g * HD:(g + 1) * HD] = gap[g * TILE:(g + 1) * TILE]


def shards(queries, keys, values, start_basis, out_weight):
    tok_rows = keys.shape[0]
    heads, _, rank = start_basis.shape
    prior = W // tok_rows
    local_gram = pl.pallas_call(
        gram_kernel,
        out_shape=jax.ShapeDtypeStruct((heads, HD, HD), F32),
        compiler_params=pltpu.CompilerParams(vmem_limit_bytes=24 << 20),
        cost_estimate=pl.CostEstimate(
            flops=2 * tok_rows * HD * HD * heads, bytes_accessed=2 << 20, transcendentals=0
        ),
        name="gram",
    )(keys)
    far = [
        (from_behind(keys, "seq", d), from_behind(values, "seq", d)) for d in range(prior, 1, -1)
    ]
    peers = lax.axis_size("seq")
    where_at = lax.axis_index("seq")
    spread = peers >= heads and peers & (peers - 1) == 0 and heads & (heads - 1) == 0
    if spread:
        total, left, bit = local_gram, heads, 1
        while bit < peers:
            if left > 1:
                left //= 2
                upper = (where_at & bit) != 0
                sent = jnp.where(upper, total[:left], total[left:])
                total = jnp.where(upper, total[left:], total[:left]) + partner(sent, "seq", bit)
            else:
                total = total + partner(total, "seq", bit)
            bit *= 2
    else:
        total = lax.psum(local_gram, "seq")
    total, keys, values, far = lax.optimization_barrier((total, keys, values, far))
    near = (from_behind(keys, "seq", 1), from_behind(values, "seq", 1))
    if spread:
        owner, left, bit = 0, heads, 1
        while left > 1:
            left //= 2
            owner = owner + jnp.where((where_at & bit) != 0, left, 0)
            bit *= 2
        start = lax.dynamic_slice_in_dim(start_basis, owner, 1, 0)
        basis_half = subspace(total, start)
        basis_half, near = lax.optimization_barrier((basis_half, near))
        while bit > 1:
            bit //= 2
            upper = (where_at & bit) != 0
            other = partner(basis_half, "seq", bit)
            basis_half = jnp.concatenate(
                [jnp.where(upper, other, basis_half), jnp.where(upper, basis_half, other)], axis=0
            )
    else:
        basis_half = subspace(total, start_basis)

    blocks = far + [near, (keys, values)]
    key_blocks, value_blocks = [b[0] for b in blocks], [b[1] for b in blocks]

    wide = pl.BlockSpec((tok_rows, GROUP * HD), lambda h: (0, h))
    narrow = pl.BlockSpec((tok_rows, HD), lambda h: (0, h))
    span = (prior + 1) * tok_rows
    lowrank_attn, gap = pl.pallas_call(
        functools.partial(attend_kernel, prior),
        grid=(heads,),
        in_specs=[wide]
        + [narrow] * (2 * prior + 2)
        + [pl.BlockSpec((1, HD, rank), lambda h: (h, 0, 0))],
        out_specs=[wide, wide],
        out_shape=[jax.ShapeDtypeStruct(queries.shape, BF16)] * 2,
        scratch_shapes=[
            pltpu.VMEM((span, HD), BF16),
            pltpu.VMEM((span, 2 * HD), BF16),
            pltpu.VMEM((span, rank), BF16),
        ],
        compiler_params=pltpu.CompilerParams(vmem_limit_bytes=48 << 20),
        cost_estimate=pl.CostEstimate(
            flops=30_000_000_000, bytes_accessed=16 << 20, transcendentals=40_000_000
        ),
        name="attend",
    )(queries, *key_blocks, *value_blocks, basis_half)

    peers = lax.axis_size("head")
    if peers == 2:
        mine = lax.axis_index("head")
        half_rows = tok_rows // 2

        def project(which):
            rows = lax.dynamic_slice_in_dim(gap, which * half_rows, half_rows, 0)
            return jnp.dot(rows, out_weight, preferred_element_type=F32).astype(BF16)

        arrived = lax.ppermute(project(1 - mine), "head", [(0, 1), (1, 0)])
        deviation = (project(mine).astype(F32) + arrived.astype(F32)).astype(BF16)
    else:
        deviation = lax.psum_scatter(
            jnp.dot(gap, out_weight, preferred_element_type=F32).astype(BF16),
            "head",
            scatter_dimension=0,
            tiled=True,
        )
    return (lowrank_attn, deviation)


def solution(mesh):
    placed = (
        P("seq", "head"),
        P("seq", "head"),
        P("seq", "head"),
        P("head", None, None),
        P("head", None),
    )
    return jax.shard_map(
        shards,
        mesh=mesh,
        in_specs=placed,
        out_specs=(P("seq", "head"), P(("seq", "head"), None)),
        check_vma=False,
    )
```
